32 devices in a mesh: dp: 16 (over z, y, x), tensor: 2 (over core).
Axes of the slice: x: 2, y: 2, z: 4, core: 2. Of those that a mesh axis runs over, the one named last changes fastest.
Arguments:
- tokens: bfloat16 [16384, 1024], P(('dp', 'tensor')), may hold values from -6 to 6
- segments: int32 [16, 1024], P('dp'), may hold values from 0 to 256, as said below
- norm1_gain: float32 [1024], replicated, may hold values from 0.25 to 1.75
- in_weight: bfloat16 [1024, 3, 1024], P(None, None, 'tensor'), may hold values from -0.1875 to 0.1875
- conv_kernel: float32 [3, 1024], P(None, 'tensor'), may hold values from -3.5 to 3.5
- out_weight: bfloat16 [1024, 1024], P('tensor'), may hold values from -0.1875 to 0.1875
- norm2_gain: float32 [1024], replicated, may hold values from 0.25 to 1.75
- gate_weight: bfloat16 [1024, 4608], P(None, 'tensor'), may hold values from -0.1875 to 0.1875
- up_weight: bfloat16 [1024, 4608], P(None, 'tensor'), may hold values from -0.1875 to 0.1875
- down_weight: bfloat16 [4608, 1024], P('tensor'), may hold values from -0.09375 to 0.09375
- cotangent: bfloat16 [16384, 1024], P(('dp', 'tensor')), may hold values from -12 to 12
Outputs:
- mixed: bfloat16 [16384, 1024], P(('dp', 'tensor'))
- input_grad: float32 [16384, 1024], P(('dp', 'tensor'))
- norm1_grad: float32 [1024], P('tensor')
- in_grad: float32 [1024, 3, 1024], P('dp', None, 'tensor')
- kernel_grad: float32 [3, 1024], P(None, 'tensor')
- out_grad: float32 [1024, 1024], P('tensor', 'dp')
- norm2_grad: float32 [1024], P('tensor')
- gate_grad: float32 [1024, 4608], P('dp', 'tensor')
- up_grad: float32 [1024, 4608], P('dp', 'tensor')
- down_grad: float32 [4608, 1024], P('tensor', 'dp')
The draws below stay inside these ranges and needn't reach their ends.
Inputs may be any that keep to these rules, and one draw needn't show every extreme that they name: `segments`: along each row the numbers start at 0, never fall and rise by at most one from a token to the next; every row ends at the largest value; in each row one document covers every position from below 512 up to 512.
All inputs are finite; a program needn't handle non-finite values.
Results may differ from the reference program's by a relative error of at most 0.018.
Values may be sent and summed in bfloat16 or wider, within the bound.
A program may use at most 192 MiB of HBM per device.

```python
import jax
import jax.numpy as jnp
from jax import lax

D = 1024
FF = 4608
KERNEL = 3
LEN = 1024
ROWS = 512
TOKENS = 16384
N_DP = 16


def segment_row(key):
    key_start, key_end, key_order = jax.random.split(key, 3)
    half_rows = ROWS // 2
    start_at = jax.random.randint(key_start, (), half_rows + 1, ROWS + 1)
    end_at = LEN - ROWS + jax.random.randint(key_end, (), 1, half_rows + 1)
    position = jnp.arange(LEN, dtype=jnp.int32)
    allowed = ((position >= 1) & ((position < start_at) | (position >= end_at))).astype(jnp.int32)
    order = jax.random.permutation(key_order, LEN).astype(jnp.int32)
    scores = order + allowed * LEN
    chosen = lax.top_k(scores, half_rows)[1].astype(jnp.int32)
    starts = jnp.sum((position[None, :] == chosen[:, None]).astype(jnp.int32), axis=0)
    return jnp.cumsum(starts).astype(jnp.int32)


def draw_segments(key, part):
    key = jax.random.fold_in(key, 11)
    row_keys = jax.random.split(key, N_DP)
    return jax.vmap(segment_row)(row_keys).astype(jnp.int32)


def draw_cotangent(key, part):
    key = jax.random.fold_in(key, 23)
    ramp = jnp.arange(TOKENS, dtype=jnp.float32)[:, None] / max(TOKENS - 1, 1)
    base = jnp.clip(jax.random.normal(key, (TOKENS, D), jnp.float32), -4.0, 4.0)
    scaled = base * jnp.exp(ramp * 1.0986123)
    return scaled.astype(jnp.bfloat16)


def levels(own_key, shape, cuts, smallest, high):
    level = 1.0
    for dim, parts in cuts:
        steps = jax.random.uniform(jax.random.fold_in(jax.random.fold_in(own_key, 6), dim), (parts,), jnp.float32, smallest / len(cuts), high / len(cuts))
        level = level * jnp.repeat(jnp.exp(steps), shape[dim] // parts).reshape((-1,) + (1,) * (len(shape) - 1 - dim))
    return level


def gaussian(stream_key, shape, scale, most, shards=(), kind=jnp.bfloat16):
    level = levels(stream_key, shape, shards, -0.22, 0.18) if shards else 1.0
    array = jax.random.normal(stream_key, shape, jnp.float32) * scale * level
    return jnp.minimum(jnp.maximum(array, -most), most).astype(kind)


def setup_inputs(seed: int = 0) -> dict:
    streams_of = jax.random.split(jax.random.key(seed), 12)
    return {
        "tokens": gaussian(streams_of[0], (TOKENS, D), 1.0, 6.0, ((0, 32),)),
        "segments": draw_segments(jax.random.fold_in(streams_of[11], 71), 0),
        "norm1_gain": jnp.clip(1.0 + 0.15 * jax.random.normal(streams_of[2], (D,), jnp.float32), 0.25, 1.75),
        "in_weight": gaussian(streams_of[3], (D, 3, D), D ** -0.5, 0.1875, ((2, 2),)),
        "conv_kernel": gaussian(streams_of[4], (KERNEL, D), KERNEL ** -0.5, 3.5, ((1, 2),), jnp.float32),
        "out_weight": gaussian(streams_of[5], (D, D), D ** -0.5, 0.1875, ((0, 2),)),
        "norm2_gain": jnp.clip(1.0 + 0.15 * jax.random.normal(streams_of[6], (D,), jnp.float32), 0.25, 1.75),
        "gate_weight": gaussian(streams_of[7], (D, FF), D ** -0.5, 0.1875, ((1, 2),)),
        "up_weight": gaussian(streams_of[8], (D, FF), D ** -0.5, 0.1875, ((1, 2),)),
        "down_weight": gaussian(streams_of[9], (FF, D), FF ** -0.5, 0.09375, ((0, 2),)),
        "cotangent": draw_cotangent(jax.random.fold_in(streams_of[11], 71), 0),
    }


EPSILON = 1e-06
HIGH = lax.Precision.HIGHEST

@jax.custom_vjp
def low(v):
    return lax.optimization_barrier(v.astype(jnp.bfloat16)).astype(jnp.float32)

@jax.custom_vjp
def low_back(v):
    return v

def low_keep(v):
    return (low(v), None)

def low_pass(kept, grad):
    return (grad,)

def back_keep(v):
    return (v, None)

def back_low(kept, grad):
    return (low(grad),)
low.defvjp(low_keep, low_pass)
low_back.defvjp(back_keep, back_low)

def normed(values, scales):
    inverse = lax.rsqrt(lax.optimization_barrier(jnp.mean(values * values, axis=-1, keepdims=True)) + EPSILON)
    return values * inverse * scales

def short_conv(gated, kernel, seg_row):
    taps = kernel.shape[0]
    summed = kernel[taps - 1] * gated
    for tap_index in range(taps - 1):
        lag_steps = taps - 1 - tap_index
        delayed = jnp.concatenate([jnp.zeros_like(gated[:lag_steps]), gated[:-lag_steps]], axis=0)
        same_doc = jnp.concatenate([jnp.zeros((lag_steps,), jnp.int32), (seg_row[lag_steps:] == seg_row[:-lag_steps]).astype(jnp.int32)])
        summed = summed + kernel[tap_index] * delayed * same_doc[:, None].astype(gated.dtype)
    return summed

def mixer_layer(inputs, seg_row, norm1_gain, in_weight, conv_kernel, out_weight, norm2_gain, gate_weight, up_weight, down_weight):
    first_norm = low(normed(inputs, norm1_gain))
    projected = low_back(jnp.einsum('td,dkc->tkc', first_norm, in_weight, precision=HIGH))
    gated = projected[:, 0] * projected[:, 2]
    conv_out = short_conv(gated, conv_kernel, seg_row)
    mixer_act = low(projected[:, 1] * conv_out)
    mixer_out = low_back(jnp.dot(mixer_act, out_weight, precision=HIGH))
    middle = inputs + mixer_out
    second_norm = low(normed(middle, norm2_gain))
    gate_val = low_back(jnp.dot(second_norm, gate_weight, precision=HIGH))
    up_val = low_back(jnp.dot(second_norm, up_weight, precision=HIGH))
    hidden = low(jax.nn.silu(gate_val) * up_val)
    ffn_out = low_back(jnp.dot(hidden, down_weight, precision=HIGH))
    return middle + ffn_out

def reference(tokens, segments, norm1_gain, in_weight, conv_kernel, out_weight, norm2_gain, gate_weight, up_weight, down_weight, cotangent):
    params = tuple((weight_arg.astype(jnp.float32) for weight_arg in (norm1_gain, in_weight, conv_kernel, out_weight, norm2_gain, gate_weight, up_weight, down_weight)))
    model_width = tokens.shape[1]
    seq_count = segments.shape[0]
    seq_len = segments.shape[1]
    inputs_all = tokens.astype(jnp.float32).reshape(seq_count, seq_len, model_width)
    cot_all = cotangent.astype(jnp.float32).reshape(seq_count, seq_len, model_width)

    def one_row(carried, element):
        inputs, seg_row, cot_row = element

        def forward(inputs_in, *weights):
            return mixer_layer(inputs_in, seg_row, *weights)
        result, pullback = jax.vjp(forward, inputs, *params)
        gradients = pullback(cot_row)
        carried = tuple((running + fresh for running, fresh in zip(carried, gradients[1:])))
        return (carried, (result.astype(jnp.bfloat16), gradients[0]))
    start_sums = tuple((jnp.zeros_like(weight_arg) for weight_arg in params))
    totals, (outputs, input_grads) = lax.scan(one_row, start_sums, (inputs_all, segments, cot_all))
    return (outputs.reshape(-1, model_width), input_grads.reshape(-1, model_width), totals[0], totals[1], totals[2], totals[3], totals[4], totals[5], totals[6], totals[7])
```

```python
import jax
import jax.numpy as jnp
from jax import lax
from jax.sharding import PartitionSpec as P

EPSILON = 1e-06


def normalize(values):
    inverse = lax.rsqrt(jnp.mean(values * values, axis=-1, keepdims=True) + EPSILON)
    return (values * inverse, inverse)


def norm_back(grad_norm, unit_rows, inverse, scales):
    grad_unit = grad_norm * scales
    grad_in = inverse * (
        grad_unit - unit_rows * jnp.mean(grad_unit * unit_rows, axis=-1, keepdims=True)
    )
    return (grad_in, jnp.sum(grad_norm * unit_rows, axis=0))


def lagged(values, lag_steps):
    return jnp.roll(values, lag_steps, axis=0)


def leading(values, lag_steps):
    return jnp.roll(values, -lag_steps, axis=0)


def doc_mask(seg_row, lag_steps):
    same_doc = jnp.concatenate(
        [
            jnp.zeros((lag_steps,), jnp.int32),
            (seg_row[lag_steps:] == seg_row[:-lag_steps]).astype(jnp.int32),
        ]
    )
    return same_doc[:, None].astype(jnp.float32)


def dot_nt(left, right):
    return lax.dot_general(
        left, right, (((1,), (1,)), ((), ())), preferred_element_type=jnp.float32
    )


def dot_tn(left, right):
    return lax.dot_general(
        left, right, (((0,), (0,)), ((), ())), preferred_element_type=jnp.float32
    )


def rotate_rows(values, steps):
    twice = jnp.concatenate([values, values], axis=0)
    return lax.dynamic_slice_in_dim(twice, steps, values.shape[0], 0)


def swap(values):
    return lax.ppermute(values, "tensor", [(0, 1), (1, 0)])


def gather_rows(values):
    size = lax.axis_size("tensor")
    if size == 2:
        return jnp.concatenate([values, swap(values)], axis=0)
    whole = lax.all_gather(values, "tensor", axis=0, tiled=True)
    return rotate_rows(whole, lax.axis_index("tensor") * values.shape[0])


def sum_rows(product, own_rows, *operands):
    size = lax.axis_size("tensor")
    if size == 2:
        theirs = product(*(operand[own_rows:] for operand in operands))
        received = swap(theirs.astype(jnp.bfloat16))
        ours = product(*(operand[:own_rows] for operand in operands))
        return ours + received.astype(jnp.float32)
    total_rows = size * own_rows
    start = lax.axis_index("tensor") * own_rows
    ordered = rotate_rows(product(*operands), lax.rem(total_rows - start, total_rows))
    return lax.psum_scatter(
        ordered.astype(jnp.bfloat16), "tensor", scatter_dimension=0, tiled=True
    ).astype(jnp.float32)


def partners(bit):
    return [(i, i ^ (1 << bit)) for i in range(lax.axis_size("dp"))]


def dp_bits():
    return lax.axis_size("dp").bit_length() - 1


def dp_orders():
    bits = dp_bits()
    if bits == 4:
        return ((0, 2, 1, 3), (1, 2, 0, 3))
    return (tuple(range(bits)), tuple(reversed(range(bits))))


def halve(part, order):
    bits = dp_bits()
    me = lax.axis_index("dp")
    rows, columns = part.shape
    part = part.reshape((2,) * bits + (rows >> bits, columns))
    left = list(reversed(range(bits)))
    for bit in order:
        axis = left.index(bit)
        mine = lax.rem(me >> bit, 2)
        sent = lax.dynamic_index_in_dim(part, 1 - mine, axis, keepdims=False)
        kept = lax.dynamic_index_in_dim(part, mine, axis, keepdims=False)
        received = lax.ppermute(sent, "dp", partners(bit))
        part = kept.astype(jnp.float32) + received.astype(jnp.float32)
        left.remove(bit)
        if left:
            part = part.astype(jnp.bfloat16)
    return part


def reduce_dp(part):
    orders = dp_orders()
    width = part.shape[1] // len(orders)
    return jnp.concatenate(
        [halve(part[:, i * width : (i + 1) * width], order) for i, order in enumerate(orders)],
        axis=1,
    )


def sum_dp(values):
    for bit in range(dp_bits()):
        values = values + lax.ppermute(values, "dp", partners(bit))
    return values


def sum_gains(gains, local_ch):
    size = lax.axis_size("tensor")
    me = lax.axis_index("tensor")
    if size == 2:
        theirs = lax.dynamic_slice_in_dim(gains, (1 - me) * local_ch, local_ch, 1)
        ours = lax.dynamic_slice_in_dim(gains, me * local_ch, local_ch, 1)
        return ours + swap(theirs)
    return lax.dynamic_slice_in_dim(lax.psum(gains, "tensor"), me * local_ch, local_ch, 1)


def local(
    tokens,
    segments,
    norm1_gain,
    in_weight,
    conv_kernel,
    out_weight,
    norm2_gain,
    gate_weight,
    up_weight,
    down_weight,
    cotangent,
):
    own_rows, width = tokens.shape
    local_ch = conv_kernel.shape[1]
    taps = conv_kernel.shape[0]
    row_start = lax.axis_index("tensor") * own_rows
    seg_row = segments[0]
    inputs = tokens.astype(jnp.float32)
    unit1, inv1 = normalize(inputs)
    norm1 = (unit1 * norm1_gain).astype(jnp.bfloat16)
    norm1_all = gather_rows(norm1)
    cot_all = gather_rows(cotangent)
    projected = jnp.einsum("td,dkc->tkc", norm1_all, in_weight, preferred_element_type=jnp.float32)
    b_gate = projected[:, 0]
    c_gate = projected[:, 1]
    x_gate = projected[:, 2]
    gated = b_gate * x_gate
    conv_out = conv_kernel[taps - 1] * gated
    masks = []
    masked_lags = []
    for tap_index in range(taps - 1):
        lag_steps = taps - 1 - tap_index
        tap_mask = rotate_rows(doc_mask(seg_row, lag_steps), row_start)
        masked = lagged(gated, lag_steps) * tap_mask
        masks.append(tap_mask)
        masked_lags.append(masked)
        conv_out = conv_out + conv_kernel[tap_index] * masked
    mixer_act = (c_gate * conv_out).astype(jnp.bfloat16)
    mixer_out = sum_rows(
        lambda act: jnp.dot(act, out_weight, preferred_element_type=jnp.float32),
        own_rows,
        mixer_act,
    )
    middle = inputs + mixer_out
    unit2, inv2 = normalize(middle)
    norm2 = (unit2 * norm2_gain).astype(jnp.bfloat16)
    norm2_all = gather_rows(norm2)
    gate_val = jnp.dot(norm2_all, gate_weight, preferred_element_type=jnp.float32)
    up_val = jnp.dot(norm2_all, up_weight, preferred_element_type=jnp.float32)
    sigma = jax.nn.sigmoid(gate_val)
    silu_val = gate_val * sigma
    hidden = (silu_val * up_val).astype(jnp.bfloat16)
    cot_rows = cotangent.astype(jnp.float32)
    down_total = reduce_dp(dot_tn(cot_all, hidden).astype(jnp.bfloat16)).T
    ffn_out = sum_rows(
        lambda act: jnp.dot(act, down_weight, preferred_element_type=jnp.float32),
        own_rows,
        hidden,
    )
    mixed = (middle + ffn_out).astype(jnp.bfloat16)
    d_hidden = dot_nt(cot_all, down_weight)
    d_gate = (d_hidden * up_val * sigma * (1.0 + gate_val * (1.0 - sigma))).astype(jnp.bfloat16)
    d_up = (d_hidden * silu_val).astype(jnp.bfloat16)
    gate_total = reduce_dp(dot_tn(norm2_all, d_gate).astype(jnp.bfloat16))
    up_total = reduce_dp(dot_tn(norm2_all, d_up).astype(jnp.bfloat16))
    d_norm2 = sum_rows(
        lambda gate, up: dot_nt(gate, gate_weight) + dot_nt(up, up_weight),
        own_rows,
        d_gate,
        d_up,
    )
    d_mid_norm, gain2_part = norm_back(d_norm2, unit2, inv2, norm2_gain)
    d_middle = cot_rows + d_mid_norm
    d_middle_all = gather_rows(d_middle.astype(jnp.bfloat16))
    d_mixer = dot_nt(d_middle_all, out_weight)
    out_total = reduce_dp(dot_tn(d_middle_all, mixer_act).astype(jnp.bfloat16)).T
    d_conv = d_mixer * c_gate
    d_c = d_mixer * conv_out
    d_gated = conv_kernel[taps - 1] * d_conv
    kernel_rows = []
    for tap_index in range(taps - 1):
        lag_steps = taps - 1 - tap_index
        d_gated = d_gated + conv_kernel[tap_index] * leading(d_conv * masks[tap_index], lag_steps)
        kernel_rows.append(jnp.sum(d_conv * masked_lags[tap_index], axis=0))
    kernel_rows.append(jnp.sum(d_conv * gated, axis=0))
    kernel_part = jnp.stack(kernel_rows, axis=0)
    d_projected = jnp.concatenate([d_gated * x_gate, d_c, d_gated * b_gate], axis=1).astype(
        jnp.bfloat16
    )
    in_total = reduce_dp(dot_tn(norm1_all, d_projected).astype(jnp.bfloat16)).reshape(
        -1, 3, local_ch
    )
    in_flat = in_weight.reshape(width, -1)
    d_norm1 = sum_rows(lambda grad: dot_nt(grad, in_flat), own_rows, d_projected)
    d_in_norm, gain1_part = norm_back(d_norm1, unit1, inv1, norm1_gain)
    input_grad = d_middle + d_in_norm
    gains = sum_gains(jnp.stack([gain1_part, gain2_part]), local_ch)
    small = sum_dp(jnp.concatenate([gains, kernel_part], axis=0))
    return (
        mixed,
        input_grad,
        small[0],
        in_total,
        small[2:],
        out_total,
        small[1],
        gate_total,
        up_total,
        down_total,
    )


def solution(mesh):
    in_specs = (
        P(("dp", "tensor"), None),
        P("dp", None),
        P(),
        P(None, None, "tensor"),
        P(None, "tensor"),
        P("tensor", None),
        P(),
        P(None, "tensor"),
        P(None, "tensor"),
        P("tensor", None),
        P(("dp", "tensor"), None),
    )
    out_specs = (
        P(("dp", "tensor"), None),
        P(("dp", "tensor"), None),
        P("tensor"),
        P("dp", None, "tensor"),
        P(None, "tensor"),
        P("tensor", "dp"),
        P("tensor"),
        P("dp", "tensor"),
        P("dp", "tensor"),
        P("tensor", "dp"),
    )
    return jax.shard_map(local, mesh=mesh, in_specs=in_specs, out_specs=out_specs, check_vma=False)
```

```python
import jax
import jax.numpy as jnp
from jax import lax
from jax.sharding import PartitionSpec as P

EPSILON = 1e-06


def normalize(values):
    inverse = lax.rsqrt(jnp.mean(values * values, axis=-1, keepdims=True) + EPSILON)
    return (values * inverse, inverse)


def norm_back(grad_norm, unit_rows, inverse, scales):
    grad_unit = grad_norm * scales
    grad_in = inverse * (
        grad_unit - unit_rows * jnp.mean(grad_unit * unit_rows, axis=-1, keepdims=True)
    )
    return (grad_in, jnp.sum(grad_norm * unit_rows, axis=0))


def lagged(values, lag_steps):
    return jnp.roll(values, lag_steps, axis=0)


def leading(values, lag_steps):
    return jnp.roll(values, -lag_steps, axis=0)


def doc_mask(seg_row, lag_steps):
    same_doc = jnp.concatenate(
        [
            jnp.zeros((lag_steps,), jnp.int32),
            (seg_row[lag_steps:] == seg_row[:-lag_steps]).astype(jnp.int32),
        ]
    )
    return same_doc[:, None].astype(jnp.float32)


def dot_nt(left, right):
    return lax.dot_general(
        left, right, (((1,), (1,)), ((), ())), preferred_element_type=jnp.float32
    )


def dot_tn(left, right):
    return lax.dot_general(
        left, right, (((0,), (0,)), ((), ())), preferred_element_type=jnp.float32
    )


def rotate_rows(values, steps):
    twice = jnp.concatenate([values, values], axis=0)
    return lax.dynamic_slice_in_dim(twice, steps, values.shape[0], 0)


def swap(values):
    return lax.ppermute(values, "tensor", [(0, 1), (1, 0)])


def gather_rows(values):
    size = lax.axis_size("tensor")
    if size == 2:
        return jnp.concatenate([values, swap(values)], axis=0)
    whole = lax.all_gather(values, "tensor", axis=0, tiled=True)
    return rotate_rows(whole, lax.axis_index("tensor") * values.shape[0])


def sum_rows(product, own_rows, *operands):
    size = lax.axis_size("tensor")
    if size == 2:
        theirs = product(*(operand[own_rows:] for operand in operands))
        received = swap(theirs.astype(jnp.bfloat16))
        ours = product(*(operand[:own_rows] for operand in operands))
        return ours + received.astype(jnp.float32)
    total_rows = size * own_rows
    start = lax.axis_index("tensor") * own_rows
    ordered = rotate_rows(product(*operands), lax.rem(total_rows - start, total_rows))
    return lax.psum_scatter(
        ordered.astype(jnp.bfloat16), "tensor", scatter_dimension=0, tiled=True
    ).astype(jnp.float32)


def partners(bit):
    return [(i, i ^ (1 << bit)) for i in range(lax.axis_size("dp"))]


def dp_bits():
    return lax.axis_size("dp").bit_length() - 1


def exchange(part, step):
    bits = dp_bits()
    size, tensors = lax.axis_size("dp"), lax.axis_size("tensor")
    odd = lax.rem(lax.axis_index("tensor"), 2)
    me = lax.axis_index("dp")
    if step > 1:
        mine = lax.rem(me >> step, 2)
        sent = lax.dynamic_index_in_dim(part, 1 - mine, bits - 1 - step, keepdims=False)
        kept = lax.dynamic_index_in_dim(part, mine, bits - 1 - step, keepdims=False)
        return kept, lax.ppermute(sent, "dp", partners(step))
    low, high = lax.rem(me, 2), lax.rem(me >> 1, 2)
    crossed = [
        ((i * tensors + t), ((i ^ (1 << (step ^ (t % 2)))) * tensors + t))
        for i in range(size)
        for t in range(tensors)
    ]
    if step == 0:
        pairs = part.reshape(part.shape[: bits - 2] + (4,) + part.shape[bits:])

        def half(own_low, own_high):
            blocks = [
                lax.dynamic_index_in_dim(
                    pairs, jnp.where(odd == 0, 2 * j + own_low, 2 * own_high + j), bits - 2
                )
                for j in range(2)
            ]
            return jnp.concatenate(blocks, axis=bits - 2)

        sent, kept = half(1 - low, 1 - high), half(low, high)
    else:
        mine = jnp.where(odd == 0, high, low)
        sent = lax.dynamic_index_in_dim(part, 1 - mine, bits - 2, keepdims=False)
        kept = lax.dynamic_index_in_dim(part, mine, bits - 2, keepdims=False)
    return kept, lax.ppermute(sent, ("dp", "tensor"), crossed)


def split_rows(part):
    bits = dp_bits()
    return part.reshape((2,) * bits + (part.shape[0] >> bits, part.shape[1]))


def add_half(halves):
    kept, received = halves
    return kept.astype(jnp.float32) + received.astype(jnp.float32)


def onward(halves, step):
    return exchange(add_half(halves).astype(jnp.bfloat16), step)


def together(values, *halves):
    values, arrived = lax.optimization_barrier((values, tuple(got for _, got in halves)))
    return values, *((kept, got) for (kept, _), got in zip(halves, arrived))


def finish(halves, step):
    for later_step in range(step, dp_bits()):
        halves = onward(halves, later_step)
    return add_half(halves)


def sum_dp(values, first_bit, end_bit):
    for bit in range(first_bit, end_bit):
        values = values + lax.ppermute(values, "dp", partners(bit))
    return values


def sum_gains(gains, local_ch):
    size = lax.axis_size("tensor")
    me = lax.axis_index("tensor")
    if size == 2:
        theirs = lax.dynamic_slice_in_dim(gains, (1 - me) * local_ch, local_ch, 1)
        ours = lax.dynamic_slice_in_dim(gains, me * local_ch, local_ch, 1)
        return ours + swap(theirs)
    return lax.dynamic_slice_in_dim(lax.psum(gains, "tensor"), me * local_ch, local_ch, 1)


def local(
    tokens,
    segments,
    norm1_gain,
    in_weight,
    conv_kernel,
    out_weight,
    norm2_gain,
    gate_weight,
    up_weight,
    down_weight,
    cotangent,
):
    own_rows, width = tokens.shape
    local_ch = conv_kernel.shape[1]
    taps = conv_kernel.shape[0]
    row_start = lax.axis_index("tensor") * own_rows
    seg_row = segments[0]
    inputs = tokens.astype(jnp.float32)
    unit1, inv1 = normalize(inputs)
    norm1 = (unit1 * norm1_gain).astype(jnp.bfloat16)
    norm1_all = gather_rows(norm1)
    cot_all = gather_rows(cotangent)
    projected = jnp.einsum("td,dkc->tkc", norm1_all, in_weight, preferred_element_type=jnp.float32)
    b_gate = projected[:, 0]
    c_gate = projected[:, 1]
    x_gate = projected[:, 2]
    gated = b_gate * x_gate
    conv_out = conv_kernel[taps - 1] * gated
    masks = []
    masked_lags = []
    for tap_index in range(taps - 1):
        lag_steps = taps - 1 - tap_index
        tap_mask = rotate_rows(doc_mask(seg_row, lag_steps), row_start)
        masked = lagged(gated, lag_steps) * tap_mask
        masks.append(tap_mask)
        masked_lags.append(masked)
        conv_out = conv_out + conv_kernel[tap_index] * masked
    mixer_act = (c_gate * conv_out).astype(jnp.bfloat16)
    mixer_out = sum_rows(
        lambda act: jnp.dot(act, out_weight, preferred_element_type=jnp.float32),
        own_rows,
        mixer_act,
    )
    middle = inputs + mixer_out
    unit2, inv2 = normalize(middle)
    norm2 = (unit2 * norm2_gain).astype(jnp.bfloat16)
    norm2_all = gather_rows(norm2)
    gate_val = jnp.dot(norm2_all, gate_weight, preferred_element_type=jnp.float32)
    up_val = jnp.dot(norm2_all, up_weight, preferred_element_type=jnp.float32)
    sigma = jax.nn.sigmoid(gate_val)
    silu_val = gate_val * sigma
    hidden = (silu_val * up_val).astype(jnp.bfloat16)
    cot_rows = cotangent.astype(jnp.float32)
    down_part = dot_tn(cot_all, hidden).astype(jnp.bfloat16)
    cot_all, down_part = lax.optimization_barrier((cot_all, down_part))
    d_hidden = dot_nt(cot_all, down_weight)
    d_gate = (d_hidden * up_val * sigma * (1.0 + gate_val * (1.0 - sigma))).astype(jnp.bfloat16)
    d_up = (d_hidden * silu_val).astype(jnp.bfloat16)
    gate_part = dot_tn(norm2_all, d_gate).astype(jnp.bfloat16)
    up_part = dot_tn(norm2_all, d_up).astype(jnp.bfloat16)
    down = exchange(split_rows(down_part), 0)
    gate = exchange(split_rows(gate_part), 0)
    (d_gate, d_up, up_part), down = together((d_gate, d_up, up_part), down)
    up = exchange(split_rows(up_part), 0)
    down = onward(down, 1)
    d_norm2 = sum_rows(
        lambda gate, up: dot_nt(gate, gate_weight) + dot_nt(up, up_weight),
        own_rows,
        d_gate,
        d_up,
    )
    d_norm2, gate = together(d_norm2, gate)
    gate = onward(gate, 1)
    d_mid_norm, gain2_part = norm_back(d_norm2, unit2, inv2, norm2_gain)
    d_middle = cot_rows + d_mid_norm
    d_middle_low = d_middle.astype(jnp.bfloat16)
    d_middle_all = gather_rows(d_middle_low)
    d_mixer = dot_nt(d_middle_all, out_weight)
    out_part = dot_tn(d_middle_all, mixer_act).astype(jnp.bfloat16)
    d_conv = d_mixer * c_gate
    d_c = d_mixer * conv_out
    d_gated = conv_kernel[taps - 1] * d_conv
    kernel_rows = []
    for tap_index in range(taps - 1):
        lag_steps = taps - 1 - tap_index
        d_gated = d_gated + conv_kernel[tap_index] * leading(d_conv * masks[tap_index], lag_steps)
        kernel_rows.append(jnp.sum(d_conv * masked_lags[tap_index], axis=0))
    kernel_rows.append(jnp.sum(d_conv * gated, axis=0))
    kernel_part = jnp.stack(kernel_rows, axis=0)
    d_projected = jnp.concatenate([d_gated * x_gate, d_c, d_gated * b_gate], axis=1).astype(
        jnp.bfloat16
    )
    d_projected, down = together(d_projected, down)
    down = onward(down, 2)
    in_part = jnp.concatenate(
        [dot_tn(norm1_all, d_projected).astype(jnp.bfloat16), out_part], axis=1
    )
    grad = exchange(split_rows(in_part), 0)
    (d_projected_all, hidden, in_part), gate, up, down = together(
        (d_projected, hidden, in_part), gate, up, down
    )
    up = onward(up, 1)
    gate = onward(gate, 2)
    down = onward(down, 3)
    in_flat = in_weight.reshape(width, -1)
    d_norm1 = sum_rows(lambda grad: dot_nt(grad, in_flat), own_rows, d_projected_all)
    d_norm1, grad, up, gate, down = together(d_norm1, grad, up, gate, down)
    grad = onward(grad, 1)
    up = onward(up, 2)
    gate = onward(gate, 3)
    down_total = finish(down, 4).T
    gate_total = finish(gate, 4)
    d_in_norm, gain1_part = norm_back(d_norm1, unit1, inv1, norm1_gain)
    input_grad = d_middle + d_in_norm
    gains = sum_gains(jnp.stack([gain1_part, gain2_part]), local_ch)
    small = sum_dp(jnp.concatenate([gains, kernel_part], axis=0), 0, 2)
    grad = onward(grad, 2)
    small, grad, up = together(small, grad, up)
    small = sum_dp(small, 2, dp_bits())
    up_total = finish(up, 3)
    in_total = finish(grad, 3)
    out_total = in_total[:, 3 * local_ch :].T
    in_total = in_total[:, : 3 * local_ch].reshape(-1, 3, local_ch)
    ffn_out = sum_rows(
        lambda act: jnp.dot(act, down_weight, preferred_element_type=jnp.float32),
        own_rows,
        hidden,
    )
    mixed = (middle + ffn_out).astype(jnp.bfloat16)
    return (
        mixed,
        input_grad,
        small[0],
        in_total,
        small[2:],
        out_total,
        small[1],
        gate_total,
        up_total,
        down_total,
    )


def solution(mesh):
    in_specs = (
        P(("dp", "tensor"), None),
        P("dp", None),
        P(),
        P(None, None, "tensor"),
        P(None, "tensor"),
        P("tensor", None),
        P(),
        P(None, "tensor"),
        P(None, "tensor"),
        P("tensor", None),
        P(("dp", "tensor"), None),
    )
    out_specs = (
        P(("dp", "tensor"), None),
        P(("dp", "tensor"), None),
        P("tensor"),
        P("dp", None, "tensor"),
        P(None, "tensor"),
        P("tensor", "dp"),
        P("tensor"),
        P("dp", "tensor"),
        P("dp", "tensor"),
        P("tensor", "dp"),
    )
    return jax.shard_map(local, mesh=mesh, in_specs=in_specs, out_specs=out_specs, check_vma=False)
```
